512 devices in a mesh: group: 16 (over y, core), member: 32 (over x, z).
Axes of the slice: x: 4, y: 8, z: 8, core: 2. Of those that a mesh axis runs over, the one named last changes fastest.
Arguments:
- heads: bfloat16 [1048576, 768], P(('group', 'member')), may hold values from -16 to 16
- new_heads: bfloat16 [1024, 768], P('group'), may hold values from -16 to 16
- vectors: bfloat16 [512, 128, 768], P(('group', 'member')), may hold values from -16 to 16
- near_ids: int32 [512, 64], P(('group', 'member')), may hold values from 0 to 65535, as said below
Outputs:
- density: float32 [1024], P('group')
- spread: float32 [1024], P('group')
- reassign: float32 [512, 64, 128], P(('group', 'member'))
The draws below stay inside these ranges and needn't reach their ends.
Inputs may be any that keep to these rules, and one draw needn't show every extreme that they name: `near_ids`: each row holds 64 different numbers; of one row at most 4 lie in one range j * 2048 to (j + 1) * 2048 - 1, and exactly 4 in some such range.
All inputs are finite; a program needn't handle non-finite values.
Results may differ from the reference program's by a relative error of at most 0.0003.
Values may be sent and summed in bfloat16 or wider, within the bound.
A program may use at most 64 MiB of HBM per device.

```python
import jax
import jax.numpy as jnp
from jax import lax

D = 768
HEAD_DEV = 2048
BLOCK = 128
NEAR = 64
GROUP_HEADS = 65536
HEADS_ALL = 1048576
POSTS_GRP = 32
NEW = 1024
SPLITS = 512
NEAR_MOST = 4


centre_total = 32


def head_labels(key):
    key = jax.random.fold_in(key, 101)
    first, second, third = jax.random.split(key, 3)
    anywhere = jax.random.randint(first, (HEADS_ALL,), 0, centre_total)
    group_of = jnp.arange(HEADS_ALL, dtype=jnp.int32) // GROUP_HEADS
    nearby = (group_of * 5 + jax.random.randint(second, (HEADS_ALL,), 0, centre_total // 4)) % centre_total
    coin = jax.random.randint(third, (HEADS_ALL,), 0, 2)
    return jnp.where(coin == 1, anywhere, nearby).astype(jnp.int32)


def head_centres(key):
    key = jax.random.fold_in(key, 103)
    first, second = jax.random.split(key, 2)
    scales = jnp.exp(jax.random.uniform(second, (centre_total, 1), jnp.float32, jnp.log(1.0), jnp.log(2.4)))
    return jax.random.truncated_normal(first, -4.0, 4.0, (centre_total, D), jnp.float32) * scales


def listed_ids(key):
    key = jax.random.fold_in(key, 107)
    keys = jax.random.split(key, 5)
    members = GROUP_HEADS // HEAD_DEV
    units = (members - 1) * NEAR_MOST
    home = jax.random.randint(keys[0], (SPLITS, 1), 0, members)
    scores = jax.random.randint(keys[1], (SPLITS, units), 0, 2 ** 20) * units + jnp.arange(units, dtype=jnp.int32)[None, :]
    order = jnp.argsort(scores, axis=1)[:, :NEAR - NEAR_MOST].astype(jnp.int32)
    other_member = (home + 1 + order // NEAR_MOST) % members
    other_rank = order % NEAR_MOST
    home_member = jnp.broadcast_to(home, (SPLITS, NEAR_MOST))
    home_rank = jnp.broadcast_to(jnp.arange(NEAR_MOST, dtype=jnp.int32)[None, :], (SPLITS, NEAR_MOST))
    member = jnp.concatenate([home_member, other_member], axis=1).astype(jnp.int32)
    rank = jnp.concatenate([home_rank, other_rank], axis=1).astype(jnp.int32)
    stride = HEAD_DEV // NEAR_MOST
    offset = jax.random.randint(keys[2], (SPLITS, members), 0, HEAD_DEV)
    jitter = jax.random.randint(keys[3], (SPLITS, NEAR), 0, stride)
    base = jnp.take_along_axis(offset, member, axis=1)
    local = (base + rank * stride + jitter) % HEAD_DEV
    ids = member * HEAD_DEV + local
    shuffle_scores = jax.random.randint(keys[4], (SPLITS, NEAR), 0, 2 ** 20) * NEAR + jnp.arange(NEAR, dtype=jnp.int32)[None, :]
    shuffle = jnp.argsort(shuffle_scores, axis=1).astype(jnp.int32)
    return jnp.take_along_axis(ids, shuffle, axis=1).astype(jnp.int32)


def chosen_heads(ids, posting, slot):
    group_of = posting // POSTS_GRP
    return (ids[posting, slot] + group_of * GROUP_HEADS).astype(jnp.int32)


def draw_heads(key, part):
    labels = head_labels(key)
    centres = head_centres(key)
    key = jax.random.fold_in(key, 7)
    noise = 0.35 * jax.random.truncated_normal(key, -4.0, 4.0, (HEADS_ALL, D), jnp.float32)
    return (centres[labels] + noise).astype(jnp.bfloat16)


def draw_new_heads(key, part):
    labels = head_labels(key)
    ids = listed_ids(key)
    centres = head_centres(key)
    key = jax.random.fold_in(key, 11)
    count = jnp.arange(NEW, dtype=jnp.int32)
    chosen = chosen_heads(ids, count // 2, count % 2)
    noise = 0.25 * jax.random.truncated_normal(key, -4.0, 4.0, (NEW, D), jnp.float32)
    return (centres[labels[chosen]] + noise).astype(jnp.bfloat16)


def draw_vectors(key, part):
    labels = head_labels(key)
    ids = listed_ids(key)
    centres = head_centres(key)
    key = jax.random.fold_in(key, 13)
    posting = jnp.broadcast_to(jnp.arange(SPLITS, dtype=jnp.int32)[:, None], (SPLITS, BLOCK))
    slot = jnp.broadcast_to((jnp.arange(BLOCK, dtype=jnp.int32) % 2)[None, :], (SPLITS, BLOCK))
    chosen = chosen_heads(ids, posting, slot)
    noise = 0.5 * jax.random.truncated_normal(key, -4.0, 4.0, (SPLITS, BLOCK, D), jnp.float32)
    return (centres[labels[chosen]] + noise).astype(jnp.bfloat16)


def draw_near_ids(key, part):
    ids = listed_ids(key)
    return ids


def setup_inputs(seed: int = 0) -> dict:
    splits = jax.random.split(jax.random.key(seed), 5)
    return {
        "heads": draw_heads(jax.random.fold_in(splits[4], 71), 0),
        "new_heads": draw_new_heads(jax.random.fold_in(splits[4], 71), 0),
        "vectors": draw_vectors(jax.random.fold_in(splits[4], 71), 0),
        "near_ids": draw_near_ids(jax.random.fold_in(splits[4], 71), 0),
    }


def reference(heads, new_heads, vectors, near_ids):
    query_sq = jnp.sum(jnp.square(new_heads.astype(jnp.float32)), axis=1)
    stacked = heads.reshape(HEADS_ALL // HEAD_DEV, HEAD_DEV, D)

    def fold(carry, block):
        block_sq = jnp.sum(jnp.square(block.astype(jnp.float32)), axis=1)
        dots = jnp.dot(new_heads, block.T, preferred_element_type=jnp.float32)
        excess = (query_sq[:, None] + block_sq[None, :] - 2.0 * dots) / D
        weight = 1.0 / jnp.square(1.0 + excess)
        return (carry[0] + jnp.sum(weight, axis=1), carry[1] + jnp.sum(weight * excess, axis=1)), None

    start = jnp.zeros((NEW,), jnp.float32)
    (total_w, total_we), unused = lax.scan(fold, (start, start), stacked)
    density = jnp.log(total_w / HEADS_ALL)
    spread = total_we / total_w

    owner_group = (jnp.arange(SPLITS) // POSTS_GRP).astype(jnp.int32)
    global_ids = (near_ids + owner_group[:, None] * GROUP_HEADS).astype(jnp.int32)
    listed = heads[global_ids].astype(jnp.float32)
    vec32 = vectors.astype(jnp.float32)
    vec_sq = jnp.sum(jnp.square(vec32), axis=2)
    head_sq = jnp.sum(jnp.square(listed), axis=2)
    dots = jnp.einsum("pbd,pkd->pkb", vec32, listed)
    reassign = (head_sq[:, :, None] + vec_sq[:, None, :] - 2.0 * dots) / D
    return density, spread, reassign
```

```python
import functools

import jax
import jax.numpy as jnp
from jax import lax
from jax.experimental import pallas as pl
from jax.experimental.pallas import tpu as pltpu
from jax.sharding import PartitionSpec as P

F32 = jnp.float32
BF16 = jnp.bfloat16
MOST = 4
NT = (((1,), (1,)), ((), ()))


def row_of(column):
    n = column.shape[0]
    return jnp.transpose(jnp.broadcast_to(column, (n, 128)))[0:1, :]


def kernel(
    shape,
    heads_hbm,
    new_ref,
    vec_ref,
    ids_ref,
    density_ref,
    spread_ref,
    reassign_ref,
    heads,
    half_sq,
    table,
    ids_all,
    row_out,
    row_in,
    part_out,
    part_in,
    sum_out,
    sum_in,
    heads_sem,
    own_sem,
    ring_send,
    ring_recv,
    twin_send,
    twin_recv,
    ids_send,
    ids_recv,
    row_send,
    row_recv,
    part_send,
    part_recv,
    sum_send,
    sum_recv,
):
    groups, members, total_heads = shape
    chips = groups // 2
    here = lax.axis_index("group")
    me = lax.axis_index("member")
    y = here // 2
    core = here % 2
    twin = y * 2 + (1 - core)
    head_dev, width = heads.shape
    block = new_ref.shape[0]
    near = ids_ref.shape[1]
    posts = vec_ref.shape[0]
    pair = 2 * block
    scale = width / 2.0

    def chip(step):
        return lax.rem(y + step + chips, chips)

    heads_copy = pltpu.make_async_copy(heads_hbm, heads, heads_sem)
    heads_copy.start()

    barrier = pltpu.get_barrier_semaphore()

    def greet_member(j, c):
        pl.semaphore_signal(
            barrier,
            inc=1,
            device_id=(here, lax.rem(me + j, members)),
            device_id_type=pl.DeviceIdType.MESH,
        )
        return c

    def greet_group(j, c):
        pl.semaphore_signal(
            barrier,
            inc=1,
            device_id=(lax.rem(here + j, groups), me),
            device_id_type=pl.DeviceIdType.MESH,
        )
        return c

    lax.fori_loop(1, members, greet_member, 0)
    lax.fori_loop(1, groups, greet_group, 0)
    pl.semaphore_wait(barrier, members - 1 + groups - 1)

    def remote(src, dst, send, recv, device):
        copy = pltpu.make_async_remote_copy(
            src_ref=src,
            dst_ref=dst,
            send_sem=send,
            recv_sem=recv,
            device_id=device,
            device_id_type=pl.DeviceIdType.MESH,
        )
        return copy

    last = chips // 2

    def base(step, way):
        if step == 0:
            return 0
        if step == last:
            return pair * (2 * last - 1)
        return pair * (1 + 2 * (step - 1) + way)

    def mine(step, way, which):
        start = pl.multiple_of(base(step, way) + which * block, block)
        if step == last:
            half = block // 2
            return table.at[pl.ds(pl.multiple_of(start + way * half, half), half)]
        return table.at[pl.ds(start, block)]

    def source(step, way):
        if step == 1:
            if step == last:
                return new_ref.at[pl.ds(way * (block // 2), block // 2)]
            return new_ref
        start = pl.multiple_of(base(step - 1, way) + core * block, block)
        if step == last:
            half = block // 2
            return table.at[pl.ds(pl.multiple_of(start + way * half, half), half)]
        return table.at[pl.ds(start, block)]

    def ring_copy(step, way):
        target = chip(1 if way == 0 else -1) * 2 + core
        return remote(
            source(step, way),
            mine(step, way, core),
            ring_send.at[step - 1, way],
            ring_recv.at[step - 1, way],
            (target, me),
        )

    def twin_copy(step, way):
        if step == 0:
            src = new_ref
        else:
            src = mine(step, way, core)
        return remote(
            src, mine(step, way, core), twin_send.at[step, way], twin_recv.at[step, way], (twin, me)
        )

    def twin_wait(step, way):
        pltpu.make_async_copy(
            mine(step, way, 1 - core), mine(step, way, 1 - core), twin_recv.at[step, way]
        ).wait()

    ring = {}
    for way in range(2):
        ring[1, way] = ring_copy(1, way)
        ring[1, way].start()
    twins = {(0, 0): twin_copy(0, 0)}
    twins[0, 0].start()
    own = pltpu.make_async_copy(new_ref, mine(0, 0, core), own_sem.at[0])
    own.start()

    ids_own = pltpu.make_async_copy(ids_ref, ids_all.at[me], ids_recv)
    ids_own.start()

    def send_ids(j, c):
        remote(
            ids_ref, ids_all.at[me], ids_send, ids_recv, (here, lax.rem(me + j, members))
        ).start()
        return c

    lax.fori_loop(1, members, send_ids, 0)

    heads_copy.wait()
    tile = 256

    def square(t, c):
        at = pl.ds(pl.multiple_of(t * tile, tile), tile)
        h = heads[at, :].astype(F32)
        half_sq[at, :] = jnp.broadcast_to(
            0.5 * jnp.sum(h * h, axis=1, keepdims=True), (tile, 128)
        )
        return c

    lax.fori_loop(0, head_dev // tile, square, 0)

    def crowding(start, count):
        blk = table[pl.ds(start, count), :]
        b32 = blk.astype(F32)
        query = row_of(0.5 * jnp.sum(b32 * b32, axis=1, keepdims=True))

        def step(t, carry):
            acc_w, acc_we = carry
            at = pl.ds(pl.multiple_of(t * tile, tile), tile)
            dots = lax.dot_general(heads[at, :], blk, NT, preferred_element_type=F32)
            hs = half_sq[at, :]
            if count > 128:
                hs = jnp.concatenate([hs] * (count // 128), axis=1)
            u = (hs + query) - dots
            r = 1.0 / (u + scale)
            w = r * r
            we = w * u
            acc_w += jnp.sum(w.reshape(tile // 8, 8, count), axis=0)
            acc_we += jnp.sum(we.reshape(tile // 8, 8, count), axis=0)
            return acc_w, acc_we

        zero = jnp.zeros((8, count), F32)
        acc_w, acc_we = lax.fori_loop(0, head_dev // tile, step, (zero, zero))
        w = (scale * scale) * jnp.sum(acc_w, axis=0, keepdims=True)
        we = scale * jnp.sum(acc_we, axis=0, keepdims=True)
        return w, we

    def send_parts(slot, step, w, we):
        part_out[slot] = jnp.concatenate([w, we], axis=1)
        if step == 0:
            pltpu.make_async_copy(part_out.at[slot], part_in.at[here], part_recv).start()
            remote(part_out.at[slot], part_in.at[here], part_send, part_recv, (twin, me)).start()
        else:
            for c in range(2):
                remote(
                    part_out.at[slot],
                    part_in.at[here],
                    part_send,
                    part_recv,
                    (chip(step) * 2 + c, me),
                ).start()

    def unit(step):
        if step == 0:
            own.wait()
            twin_wait(0, 0)
            w, we = crowding(0, pair)
            send_parts(0, 0, w, we)
        elif step == last:
            for way in range(2):
                twin_wait(step, way)
            w, we = crowding(base(step, 0), pair)
            send_parts(2 * last - 1, step, w, we)
        else:
            for way in range(2):
                twin_wait(step, way)
            w, we = crowding(base(step, 0), 2 * pair)
            for way in range(2):
                lanes = slice(way * pair, (way + 1) * pair)
                send_parts(
                    1 + 2 * (step - 1) + way,
                    -step if way == 0 else step,
                    w[:, lanes],
                    we[:, lanes],
                )

    def arrive(step):
        for way in range(2):
            ring[step, way].wait_recv()
            if step < last:
                ring[step + 1, way] = ring_copy(step + 1, way)
                ring[step + 1, way].start()
            twins[step, way] = twin_copy(step, way)
            twins[step, way].start()

    def pick_rows():
        pltpu.make_async_copy(ids_all, ids_all, ids_recv).wait()
        ids = ids_all[:, 0, :]
        owner = ids // head_dev
        local = (ids - owner * head_dev).astype(F32)
        held = owner == me
        before = (
            lax.broadcasted_iota(jnp.int32, (near, near), 0)
            < lax.broadcasted_iota(jnp.int32, (near, near), 1)
        ).astype(F32)
        rank = jnp.dot(
            held.astype(F32).astype(BF16), before.astype(BF16), preferred_element_type=F32
        )
        columns = []
        for r in range(MOST):
            hit = jnp.where(held & (rank == float(r)), local + 1.0, 0.0)
            columns.append(jnp.sum(hit, axis=1, keepdims=True) - 1.0)
        column = jnp.concatenate(columns, axis=0)
        slots = MOST * members
        picked = jnp.zeros((slots, width), F32)
        for t in range(head_dev // tile):
            lane = (lax.broadcasted_iota(jnp.int32, (slots, tile), 1) + t * tile).astype(F32)
            onehot = (lane == column).astype(F32).astype(BF16)
            picked += jnp.dot(
                onehot, heads[t * tile : (t + 1) * tile, :], preferred_element_type=F32
            )
        picked = picked.astype(BF16)
        cut = row_out.shape[2]
        place = lax.broadcasted_iota(jnp.int32, (members * 16, slots), 0)
        slot = lax.broadcasted_iota(jnp.int32, (members * 16, slots), 1)
        target = lax.rem(slot, members) * 16 + slot // members
        packed = jnp.zeros((members * 16, cut), F32)
        for c in range(width // cut):
            move = (place == target + MOST * c).astype(F32).astype(BF16)
            packed += jnp.dot(
                move, picked[:, c * cut : (c + 1) * cut], preferred_element_type=F32
            )
        row_out[...] = packed.astype(BF16).reshape(members, 16, cut)
        pltpu.make_async_copy(row_out.at[me], row_in.at[me], row_recv).start()

        def send(j, c):
            to = lax.rem(me + j, members)
            remote(row_out.at[to], row_in.at[me], row_send, row_recv, (here, to)).start()
            return c

        lax.fori_loop(1, members, send, 0)

    def finish_rows():
        pltpu.make_async_copy(row_in, row_in, row_recv).wait()
        cut = row_in.shape[2]
        owner = jnp.broadcast_to((ids_ref[...] // head_dev).astype(F32), (near, near))
        i = lax.broadcasted_iota(jnp.int32, (near, near), 0)
        j = lax.broadcasted_iota(jnp.int32, (near, near), 1)
        column = jnp.sum(jnp.where(i == j, owner, 0.0), axis=1, keepdims=True)
        rank = jnp.sum(
            jnp.where((owner == column) & (j < i), 1.0, 0.0), axis=1, keepdims=True
        )
        got = row_in[...].reshape(members * 16, cut)
        lane = lax.broadcasted_iota(jnp.int32, (near, members * 16), 1).astype(F32)
        want = column * 16.0 + rank
        dots = jnp.zeros((near, posts), F32)
        row_sq = jnp.zeros((near, 1), F32)
        vec_sq = jnp.zeros((posts, 1), F32)
        for c in range(width // cut):
            choose = (lane == want + float(MOST * c)).astype(F32).astype(BF16)
            rows = jnp.dot(choose, got, preferred_element_type=F32)
            vec = vec_ref[:, c * cut : (c + 1) * cut]
            v32 = vec.astype(F32)
            row_sq += jnp.sum(rows * rows, axis=1, keepdims=True)
            vec_sq += jnp.sum(v32 * v32, axis=1, keepdims=True)
            dots += lax.dot_general(rows.astype(BF16), vec, NT, preferred_element_type=F32)
        reassign_ref[...] = (row_sq + row_of(vec_sq) - 2.0 * dots) / width

    arrive(1)
    unit(0)
    pick_rows()
    for step in range(2, last + 1):
        arrive(step)
        unit(step - 1)
    unit(last)

    pltpu.make_async_copy(part_in, part_in, part_recv).wait()
    sum_out[...] = jnp.sum(part_in[...], axis=0)
    pltpu.make_async_copy(sum_out, sum_in.at[me], sum_recv).start()

    def send_sum(j, c):
        remote(sum_out, sum_in.at[me], sum_send, sum_recv, (here, lax.rem(me + j, members))).start()
        return c

    lax.fori_loop(1, members, send_sum, 0)
    finish_rows()
    pltpu.make_async_copy(sum_in, sum_in, sum_recv).wait()
    total = jnp.sum(sum_in[...], axis=0)
    w = total[:, 0:pair]
    we = total[:, pair : 2 * pair]
    w = jnp.where(core == 0, w[:, 0:block], w[:, block:pair])
    we = jnp.where(core == 0, we[:, 0:block], we[:, block:pair])
    density_ref[...] = jnp.log(w / float(total_heads))
    spread_ref[...] = we / w

    for copy in ring.values():
        copy.wait_send()
    for copy in twins.values():
        copy.wait_send()
    others = pl.ds(0, members - 1)
    pltpu.make_async_copy(ids_all.at[others], ids_all.at[others], ids_send).wait()
    pltpu.make_async_copy(row_in.at[others], row_in.at[others], row_send).wait()
    pltpu.make_async_copy(sum_in.at[others], sum_in.at[others], sum_send).wait()
    others = pl.ds(0, groups - 1)
    pltpu.make_async_copy(part_in.at[others], part_in.at[others], part_send).wait()


def per_device(heads, new_heads, vectors, near_ids):
    groups = lax.axis_size("group")
    members = lax.axis_size("member")
    head_dev, width = heads.shape
    block = new_heads.shape[0]
    posts = vectors.shape[1]
    near = near_ids.shape[1]
    last = groups // 4
    vmem = pl.BlockSpec(memory_space=pltpu.VMEM)
    dma = pltpu.SemaphoreType.DMA
    density, spread, reassign = pl.pallas_call(
        functools.partial(kernel, (groups, members, head_dev * groups * members)),
        out_shape=(
            jax.ShapeDtypeStruct((1, block), F32),
            jax.ShapeDtypeStruct((1, block), F32),
            jax.ShapeDtypeStruct((near, posts), F32),
        ),
        in_specs=[pl.BlockSpec(memory_space=pl.ANY), vmem, vmem, vmem],
        out_specs=(vmem, vmem, vmem),
        scratch_shapes=[
            pltpu.VMEM((head_dev, width), BF16),
            pltpu.VMEM((head_dev, 128), F32),
            pltpu.VMEM((groups * block, width), BF16),
            pltpu.VMEM((members, 1, near), jnp.int32),
            pltpu.VMEM((members, 16, 256), BF16),
            pltpu.VMEM((members, 16, 256), BF16),
            pltpu.VMEM((groups // 2, 1, 4 * block), F32),
            pltpu.VMEM((groups, 1, 4 * block), F32),
            pltpu.VMEM((1, 4 * block), F32),
            pltpu.VMEM((members, 1, 4 * block), F32),
            dma,
            dma((1,)),
            dma((last, 2)),
            dma((last, 2)),
            dma((last + 1, 2)),
            dma((last + 1, 2)),
            dma, dma, dma, dma, dma, dma, dma, dma,
        ],
        compiler_params=pltpu.CompilerParams(
            collective_id=0, has_side_effects=True, vmem_limit_bytes=40 * 1024 * 1024
        ),
    )(heads, new_heads, vectors[0], near_ids)
    return density[0], spread[0], reassign[None]


def solution(mesh):
    placed = (
        P(("group", "member"), None),
        P("group", None),
        P(("group", "member"), None, None),
        P(("group", "member"), None),
    )
    return jax.shard_map(
        per_device,
        mesh=mesh,
        in_specs=placed,
        out_specs=(P("group"), P("group"), P(("group", "member"), None, None)),
        check_vma=False,
    )
```

```python
import functools

import jax
import jax.numpy as jnp
from jax import lax
from jax.experimental import pallas as pl
from jax.experimental.pallas import tpu as pltpu
from jax.sharding import PartitionSpec as P

F32 = jnp.float32
BF16 = jnp.bfloat16
MOST = 4
SHADES = 4
SLOTS = (0, -1, 1, -2, 2, -3, 3, 4)
ACROSS = 7
NT = (((1,), (1,)), ((), ()))


def row_of(column):
    n = column.shape[0]
    return jnp.transpose(jnp.broadcast_to(column, (n, 128)))[0:1, :]


def kernel(
    shape,
    heads_hbm,
    new_ref,
    vec_hbm,
    ids_hbm,
    density_ref,
    spread_ref,
    reassign_ref,
    heads,
    vec_ref,
    ids_ref,
    half_sq,
    table,
    ids_all,
    row_out,
    row_in,
    part_out,
    part_in,
    sum_out,
    sum_in,
    heads_sem,
    own_sem,
    ring_send,
    ring_recv,
    side_send,
    side_recv,
    twin_send,
    twin_recv,
    line_send,
    line_recv,
    ids_send,
    ids_recv,
    know_x,
    know_z,
    row_send,
    row_recv,
    part_send,
    part_recv,
    sum_send,
    sum_recv,
):
    groups, members, depth, total_heads = shape
    chips = groups // 2
    across = members // depth
    here = lax.axis_index("group")
    me = lax.axis_index("member")
    y = here // 2
    core = here % 2
    x = me // depth
    z = me % depth
    twin = y * 2 + (1 - core)
    head_dev, width = heads.shape
    block = new_ref.shape[0]
    near = ids_ref.shape[1]
    posts = vec_ref.shape[0]
    pair = 2 * block
    scale = width / 2.0
    shade = lax.rem(x + 2 * z, SHADES)
    piece = block // SHADES

    def chip(step):
        return lax.rem(y + step + chips, chips)

    def beside_x(step):
        return (here, lax.rem(x + step + across, across) * depth + z)

    def beside_z(step):
        return (here, x * depth + lax.rem(z + step + depth, depth))

    def signal(sem, device):
        pl.semaphore_signal(sem, inc=1, device_id=device, device_id_type=pl.DeviceIdType.MESH)

    def remote(src, dst, send, recv, device):
        return pltpu.make_async_remote_copy(
            src_ref=src,
            dst_ref=dst,
            send_sem=send,
            recv_sem=recv,
            device_id=device,
            device_id_type=pl.DeviceIdType.MESH,
        )

    barrier = pltpu.get_barrier_semaphore()
    for device in (
        (chip(1) * 2 + core, me),
        (chip(-1) * 2 + core, me),
        (chip(2) * 2 + core, me),
        (chip(-2) * 2 + core, me),
        (twin, me),
        beside_z(1),
        beside_z(-1),
        beside_x(1),
        beside_x(-1),
    ):
        signal(barrier, device)

    heads_copy = pltpu.make_async_copy(heads_hbm, heads, heads_sem)
    own = pltpu.make_async_copy(
        new_ref, table.at[pl.ds(pl.multiple_of(core * block, block), block)], own_sem.at[0]
    )
    own_vec = pltpu.make_async_copy(vec_hbm, vec_ref, own_sem.at[1])
    own_ids = pltpu.make_async_copy(ids_hbm, ids_ref, own_sem.at[2])
    own_ids.start()
    own.start()
    heads_copy.start()
    own_vec.start()

    def rows_at(slot, which, first, count):
        start = pl.multiple_of(slot * pair + which * block + first, 16)
        return table.at[pl.ds(start, count)]

    def hop(src, slot, step):
        remote(
            src,
            rows_at(slot, core, shade * piece, piece),
            ring_send,
            ring_recv.at[slot],
            (chip(step) * 2 + core, me),
        ).start()

    def first_hop(slot):
        hop(new_ref.at[pl.ds(pl.multiple_of(shade * piece, 16), piece)], slot, -SLOTS[slot])

    def next_hop(slot, after, step):
        hop(rows_at(slot, core, shade * piece, piece), after, step)

    def arrive(slot):
        mine = rows_at(slot, core, shade * piece, piece)
        pltpu.make_async_copy(mine, mine, ring_recv.at[slot]).wait()

    def spread_out(slot):
        mine = rows_at(slot, core, shade * piece, piece)
        if slot == ACROSS:
            way = 1 - 2 * core
        else:
            way = -1 if SLOTS[slot] > 0 else 1
        for device in (beside_x(1), beside_x(-1), beside_z(way)):
            remote(mine, mine, side_send, side_recv.at[slot], device).start()

    def give_twin(slot):
        others = rows_at(slot, core, 0, block - piece)
        pltpu.make_async_copy(others, others, side_recv.at[slot]).wait()
        whole = rows_at(slot, core, 0, block)
        remote(whole, whole, twin_send, twin_recv.at[slot], (twin, me)).start()

    def twin_wait(slot):
        there = rows_at(slot, 1 - core, 0, block)
        pltpu.make_async_copy(there, there, twin_recv.at[slot]).wait()

    pl.semaphore_wait(barrier, 9)

    for slot in (1, 2, 3, 4):
        first_hop(slot)
    signal(know_x, beside_x(-1))
    for way in (1, -1):
        signal(know_z.at[0], beside_z(way))

    line_own = pltpu.make_async_copy(ids_hbm, ids_all.at[z, x], line_recv)
    line_own.start()

    def send_line(step):
        remote(ids_hbm, ids_all.at[z, x], line_send, line_recv, beside_x(step)).start()

    send_line(1)
    send_line(-1)
    remote(new_ref, rows_at(0, core, 0, block), twin_send, twin_recv.at[0], (twin, me)).start()
    pl.semaphore_wait(know_x, 1)
    for step in range(2, across - 1):
        send_line(step)
    pl.semaphore_wait(know_z.at[0], 2)
    for way in (1, -1):
        signal(know_z.at[1], beside_z(way))

    def square_heads():
        heads_copy.wait()

        def square(t, c):
            at = pl.ds(pl.multiple_of(t * tile, tile), tile)
            h = heads[at, :].astype(F32)
            half_sq[at, :] = jnp.broadcast_to(
                0.5 * jnp.sum(h * h, axis=1, keepdims=True), (tile, 128)
            )
            return c

        lax.fori_loop(0, head_dev // tile, square, 0)

    def know_all():
        pl.semaphore_wait(know_z.at[1], 2)
        for way in (1, -1):
            signal(know_z.at[2], beside_z(way))

    def send_lists():
        pltpu.make_async_copy(ids_all.at[z], ids_all.at[z], line_recv).wait()
        pl.semaphore_wait(know_z.at[2], 2)

        def send(j, c):
            remote(ids_all.at[z], ids_all.at[z], ids_send, ids_recv, beside_z(j)).start()
            return c

        lax.fori_loop(1, depth, send, 0)

    tile = 256

    def crowding(start, count):
        blk = table[pl.ds(start, count), :]
        b32 = blk.astype(F32)
        query = row_of(0.5 * jnp.sum(b32 * b32, axis=1, keepdims=True))
        acc_w = jnp.zeros((8, count), F32)
        acc_we = jnp.zeros((8, count), F32)
        for t in range(0, head_dev, 512):
            dots = lax.dot_general(
                heads[t : t + 512, :], blk, NT, preferred_element_type=F32
            )
            hs = jnp.concatenate([half_sq[t : t + 512, :]] * (count // 128), axis=1)
            u = (hs + query) - dots
            r = 1.0 / (u + scale)
            w = r * r
            we = w * u
            acc_w += jnp.sum(w.reshape(512 // 8, 8, count), axis=0)
            acc_we += jnp.sum(we.reshape(512 // 8, 8, count), axis=0)
        w = (scale * scale) * jnp.sum(acc_w, axis=0, keepdims=True)
        we = scale * jnp.sum(acc_we, axis=0, keepdims=True)
        return w, we

    def send_parts(slot, w, we):
        part_out[slot] = jnp.concatenate([w, we], axis=1)
        if slot == 0:
            pltpu.make_async_copy(part_out.at[slot], part_in.at[here], part_recv).start()
            remote(part_out.at[slot], part_in.at[here], part_send, part_recv, (twin, me)).start()
        else:
            for c in range(2):
                remote(
                    part_out.at[slot],
                    part_in.at[here],
                    part_send,
                    part_recv,
                    (chip(SLOTS[slot]) * 2 + c, me),
                ).start()

    def unit(first, count):
        w, we = crowding(first * pair, count * pair)
        for i in range(count):
            lanes = slice(i * pair, (i + 1) * pair)
            send_parts(first + i, w[:, lanes], we[:, lanes])

    def pick_rows():
        others = ids_all.at[pl.ds(0, depth - 1)]
        pltpu.make_async_copy(others, others, ids_recv).wait()
        ids = ids_all[...].reshape(members, near)
        owner = ids // head_dev
        local = (ids - owner * head_dev).astype(F32)
        held = owner == me
        before = (
            lax.broadcasted_iota(jnp.int32, (near, near), 0)
            < lax.broadcasted_iota(jnp.int32, (near, near), 1)
        ).astype(F32)
        rank = jnp.dot(
            held.astype(F32).astype(BF16), before.astype(BF16), preferred_element_type=F32
        )
        columns = []
        for r in range(MOST):
            hit = jnp.where(held & (rank == float(r)), local + 1.0, 0.0)
            columns.append(jnp.sum(hit, axis=1, keepdims=True) - 1.0)
        column = jnp.concatenate(columns, axis=0)
        slots = MOST * members
        picked = jnp.zeros((slots, width), F32)
        for t in range(head_dev // tile):
            lane = (lax.broadcasted_iota(jnp.int32, (slots, tile), 1) + t * tile).astype(F32)
            onehot = (lane == column).astype(F32).astype(BF16)
            picked += jnp.dot(
                onehot, heads[t * tile : (t + 1) * tile, :], preferred_element_type=F32
            )
        picked = picked.astype(BF16)
        cut = row_out.shape[2]
        place = lax.broadcasted_iota(jnp.int32, (members * 16, slots), 0)
        slot = lax.broadcasted_iota(jnp.int32, (members * 16, slots), 1)
        target = lax.rem(slot, members) * 16 + slot // members
        packed = jnp.zeros((members * 16, cut), F32)
        for c in range(width // cut):
            move = (place == target + MOST * c).astype(F32).astype(BF16)
            packed += jnp.dot(
                move, picked[:, c * cut : (c + 1) * cut], preferred_element_type=F32
            )
        row_out[...] = packed.astype(BF16).reshape(members, 16, cut)
        pltpu.make_async_copy(row_out.at[z * across + x], row_in.at[me], row_recv).start()

        def send(j, c):
            to = lax.rem(me + j, members)
            at = lax.rem(to, depth) * across + to // depth
            remote(row_out.at[at], row_in.at[me], row_send, row_recv, (here, to)).start()
            return c

        lax.fori_loop(1, members, send, 0)

    def finish_rows():
        own_ids.wait()
        own_vec.wait()
        pltpu.make_async_copy(row_in, row_in, row_recv).wait()
        cut = row_in.shape[2]
        owner = jnp.broadcast_to((ids_ref[...] // head_dev).astype(F32), (near, near))
        i = lax.broadcasted_iota(jnp.int32, (near, near), 0)
        j = lax.broadcasted_iota(jnp.int32, (near, near), 1)
        column = jnp.sum(jnp.where(i == j, owner, 0.0), axis=1, keepdims=True)
        rank = jnp.sum(
            jnp.where((owner == column) & (j < i), 1.0, 0.0), axis=1, keepdims=True
        )
        got = row_in[...].reshape(members * 16, cut)
        lane = lax.broadcasted_iota(jnp.int32, (near, members * 16), 1).astype(F32)
        want = column * 16.0 + rank
        dots = jnp.zeros((near, posts), F32)
        row_sq = jnp.zeros((near, 1), F32)
        vec_sq = jnp.zeros((posts, 1), F32)
        for c in range(width // cut):
            choose = (lane == want + float(MOST * c)).astype(F32).astype(BF16)
            rows = jnp.dot(choose, got, preferred_element_type=F32)
            vec = vec_ref[:, c * cut : (c + 1) * cut]
            v32 = vec.astype(F32)
            row_sq += jnp.sum(rows * rows, axis=1, keepdims=True)
            vec_sq += jnp.sum(v32 * v32, axis=1, keepdims=True)
            dots += lax.dot_general(rows.astype(BF16), vec, NT, preferred_element_type=F32)
        reassign_ref[...] = (row_sq + row_of(vec_sq) - 2.0 * dots) / width

    square_heads()
    for slot, after, step in ((1, 5, 2), (2, 6, -2)):
        arrive(slot)
        spread_out(slot)
        next_hop(slot, after, step)
    know_all()
    for slot in (3, 4):
        arrive(slot)
        spread_out(slot)
    next_hop(3 + core, ACROSS, 2 - 4 * core)
    send_lists()
    for slot in (1, 2, 3, 4):
        give_twin(slot)
    for slot in (5, 6, ACROSS):
        arrive(slot)
        spread_out(slot)
    own.wait()
    for slot in range(4):
        twin_wait(slot)
    unit(0, 4)
    for slot in (5, 6, ACROSS):
        give_twin(slot)
    pick_rows()
    for slot in range(4, 8):
        twin_wait(slot)
    unit(4, 4)

    pltpu.make_async_copy(part_in, part_in, part_recv).wait()
    sum_out[...] = jnp.sum(part_in[...], axis=0)
    pltpu.make_async_copy(sum_out, sum_in.at[me], sum_recv).start()

    def send_sum(j, c):
        remote(sum_out, sum_in.at[me], sum_send, sum_recv, (here, lax.rem(me + j, members))).start()
        return c

    lax.fori_loop(1, members, send_sum, 0)
    finish_rows()
    pltpu.make_async_copy(sum_in, sum_in, sum_recv).wait()
    total = jnp.sum(sum_in[...], axis=0)
    w = total[:, 0:pair]
    we = total[:, pair : 2 * pair]
    w = jnp.where(core == 0, w[:, 0:block], w[:, block:pair])
    we = jnp.where(core == 0, we[:, 0:block], we[:, block:pair])
    density_ref[...] = jnp.log(w / float(total_heads))
    spread_ref[...] = we / w

    for sem, count in ((ring_send, 7 * piece), (side_send, 21 * piece), (twin_send, 8 * block)):
        sent = table.at[pl.ds(0, count)]
        pltpu.make_async_copy(sent, sent, sem).wait()
    others = pl.ds(0, members - 1)
    lines = ids_all.at[0, pl.ds(0, across - 1)]
    pltpu.make_async_copy(lines, lines, line_send).wait()
    lists = ids_all.at[pl.ds(0, depth - 1)]
    pltpu.make_async_copy(lists, lists, ids_send).wait()
    pltpu.make_async_copy(row_in.at[others], row_in.at[others], row_send).wait()
    pltpu.make_async_copy(sum_in.at[others], sum_in.at[others], sum_send).wait()
    others = pl.ds(0, groups - 1)
    pltpu.make_async_copy(part_in.at[others], part_in.at[others], part_send).wait()


def per_device(heads, new_heads, vectors, near_ids):
    groups = lax.axis_size("group")
    members = lax.axis_size("member")
    head_dev, width = heads.shape
    block = new_heads.shape[0]
    posts = vectors.shape[1]
    near = near_ids.shape[1]
    depth = 8
    anywhere = pl.BlockSpec(memory_space=pltpu.HBM)
    vmem = pl.BlockSpec(memory_space=pltpu.VMEM)
    dma = pltpu.SemaphoreType.DMA
    density, spread, reassign = pl.pallas_call(
        functools.partial(kernel, (groups, members, depth, head_dev * groups * members)),
        out_shape=(
            jax.ShapeDtypeStruct((1, block), F32),
            jax.ShapeDtypeStruct((1, block), F32),
            jax.ShapeDtypeStruct((near, posts), F32),
        ),
        in_specs=[anywhere] * 4,
        out_specs=(vmem, vmem, vmem),
        scratch_shapes=[
            pltpu.VMEM((head_dev, width), BF16),
            pltpu.VMEM((posts, width), BF16),
            pltpu.VMEM((1, near), jnp.int32),
            pltpu.VMEM((head_dev, 128), F32),
            pltpu.VMEM((groups * block, width), BF16),
            pltpu.VMEM((depth, members // depth, 1, near), jnp.int32),
            pltpu.VMEM((members, 16, 256), BF16),
            pltpu.VMEM((members, 16, 256), BF16),
            pltpu.VMEM((groups // 2, 1, 4 * block), F32),
            pltpu.VMEM((groups, 1, 4 * block), F32),
            pltpu.VMEM((1, 4 * block), F32),
            pltpu.VMEM((members, 1, 4 * block), F32),
            dma,
            dma((3,)),
            dma,
            dma((8,)),
            dma,
            dma((8,)),
            dma,
            dma((8,)),
            dma,
            dma,
            dma,
            dma,
            pltpu.SemaphoreType.REGULAR,
            pltpu.SemaphoreType.REGULAR((3,)),
            dma,
            dma,
            dma,
            dma,
            dma,
            dma,
        ],
        compiler_params=pltpu.CompilerParams(
            collective_id=0, has_side_effects=True, vmem_limit_bytes=60 * 1024 * 1024
        ),
    )(heads, new_heads, vectors[0], near_ids)
    return density[0], spread[0], reassign[None]


def solution(mesh):
    placed = (
        P(("group", "member"), None),
        P("group", None),
        P(("group", "member"), None, None),
        P(("group", "member"), None),
    )
    return jax.shard_map(
        per_device,
        mesh=mesh,
        in_specs=placed,
        out_specs=(P("group"), P("group"), P(("group", "member"), None, None)),
        check_vma=False,
    )
```

```python
import functools

import jax
import jax.numpy as jnp
from jax import lax
from jax.experimental import pallas as pl
from jax.experimental.pallas import tpu as pltpu
from jax.sharding import PartitionSpec as P

F32 = jnp.float32
BF16 = jnp.bfloat16
MOST = 4
SHADES = 4
SLOTS = (0, -1, 1, -2, 2, -3, 3, 4)
ACROSS = 7
NT = (((1,), (1,)), ((), ()))


def row_of(column):
    n = column.shape[0]
    return jnp.transpose(jnp.broadcast_to(column, (n, 128)))[0:1, :]


def kernel(
    shape,
    heads_hbm,
    new_ref,
    vec_hbm,
    ids_hbm,
    result_ref,
    heads,
    vec_ref,
    ids_ref,
    half_sq,
    table,
    ids_all,
    row_out,
    row_in,
    part_out,
    part_in,
    sum_out,
    sum_in,
    heads_sem,
    own_sem,
    ring_send,
    ring_recv,
    side_send,
    side_recv,
    twin_send,
    twin_recv,
    line_send,
    line_recv,
    ids_send,
    ids_recv,
    know_x,
    know_z,
    row_send,
    row_recv,
    part_send,
    part_recv,
    sum_send,
    sum_recv,
):
    groups, members, depth, total_heads = shape
    chips = groups // 2
    across = members // depth
    here = lax.axis_index("group")
    me = lax.axis_index("member")
    y = here // 2
    core = here % 2
    x = me // depth
    z = me % depth
    twin = y * 2 + (1 - core)
    head_dev, width = heads_hbm.shape
    block = new_ref.shape[0]
    near = ids_ref.shape[1]
    posts = vec_ref.shape[0]
    scale = width / 2.0
    far_first = sorted(
        [(i, j) for i in range(across) for j in range(depth) if i or j],
        key=lambda d: -min(d[0], across - d[0]) - min(d[1], depth - d[1]),
    )
    shade = lax.rem(x + 2 * z, SHADES)
    piece = block // SHADES

    def chip(step):
        return lax.rem(y + step + chips, chips)

    def beside_x(step):
        return (here, lax.rem(x + step + across, across) * depth + z)

    def beside_z(step):
        return (here, x * depth + lax.rem(z + step + depth, depth))

    def signal(sem, device):
        pl.semaphore_signal(sem, inc=1, device_id=device, device_id_type=pl.DeviceIdType.MESH)

    def remote(src, dst, send, recv, device):
        return pltpu.make_async_remote_copy(
            src_ref=src,
            dst_ref=dst,
            send_sem=send,
            recv_sem=recv,
            device_id=device,
            device_id_type=pl.DeviceIdType.MESH,
        )

    barrier = pltpu.get_barrier_semaphore()
    for device in (
        (chip(1) * 2 + core, me),
        (chip(-1) * 2 + core, me),
        (chip(2) * 2 + core, me),
        (chip(-2) * 2 + core, me),
        (twin, me),
        beside_z(1),
        beside_z(-1),
        beside_x(1),
        beside_x(-1),
    ):
        signal(barrier, device)

    held = pl.multiple_of(core * head_dev, head_dev)
    twin_held = pl.multiple_of((1 - core) * head_dev, head_dev)
    heads_copy = pltpu.make_async_copy(heads_hbm, heads.at[pl.ds(held, head_dev)], heads_sem)
    own = pltpu.make_async_copy(new_ref, table.at[pl.ds(0, block)], own_sem.at[0])
    own_vec = pltpu.make_async_copy(vec_hbm, vec_ref, own_sem.at[1])
    own_ids = pltpu.make_async_copy(ids_hbm, ids_ref, own_sem.at[2])
    own_ids.start()
    own.start()
    heads_copy.start()
    own_vec.start()

    def rows_at(slot, first, count):
        return table.at[pl.ds(pl.multiple_of(slot * block + first, 16), count)]

    def hop(src, slot, step):
        remote(
            src,
            rows_at(slot, shade * piece, piece),
            ring_send,
            ring_recv.at[slot],
            (chip(step) * 2 + core, me),
        ).start()

    def first_hop(slot):
        hop(new_ref.at[pl.ds(pl.multiple_of(shade * piece, 16), piece)], slot, -SLOTS[slot])

    def next_hop(slot, after, step):
        hop(rows_at(slot, shade * piece, piece), after, step)

    def arrive(slot):
        mine = rows_at(slot, shade * piece, piece)
        pltpu.make_async_copy(mine, mine, ring_recv.at[slot]).wait()

    def spread_out(slot):
        mine = rows_at(slot, shade * piece, piece)
        if slot == ACROSS:
            way = 1 - 2 * core
        else:
            way = -1 if SLOTS[slot] > 0 else 1
        for device in (beside_x(1), beside_x(-1), beside_z(way)):
            remote(mine, mine, side_send, side_recv.at[slot], device).start()

    def whole(slot):
        others = rows_at(slot, 0, block - piece)
        pltpu.make_async_copy(others, others, side_recv.at[slot]).wait()

    pl.semaphore_wait(barrier, 9)

    for slot in (3, 4, 1, 2):
        first_hop(slot)
    signal(know_x, beside_x(-1))
    for way in (1, -1):
        signal(know_z.at[0], beside_z(way))

    line_own = pltpu.make_async_copy(ids_hbm, ids_all.at[z, x], line_recv)
    line_own.start()

    def send_line(step):
        remote(ids_hbm, ids_all.at[z, x], line_send, line_recv, beside_x(step)).start()

    send_line(1)
    send_line(-1)
    twin_heads = remote(
        heads_hbm, heads.at[pl.ds(held, head_dev)], twin_send, twin_recv, (twin, me)
    )
    twin_heads.start()
    pl.semaphore_wait(know_x, 1)
    for step in range(2, across - 1):
        send_line(step)
    pl.semaphore_wait(know_z.at[0], 2)
    for way in (1, -1):
        signal(know_z.at[1], beside_z(way))

    def square_heads(first):
        def square(t, c):
            at = pl.ds(pl.multiple_of(first + t * tile, tile), tile)
            h = heads[at, :].astype(F32)
            half_sq[at, :] = jnp.broadcast_to(
                0.5 * jnp.sum(h * h, axis=1, keepdims=True), (tile, 128)
            )
            return c

        lax.fori_loop(0, head_dev // tile, square, 0)

    def know_all():
        pl.semaphore_wait(know_z.at[1], 2)
        for way in (1, -1):
            signal(know_z.at[2], beside_z(way))

    def send_lists():
        pltpu.make_async_copy(ids_all.at[z], ids_all.at[z], line_recv).wait()
        pl.semaphore_wait(know_z.at[2], 2)

        def send(j, c):
            remote(ids_all.at[z], ids_all.at[z], ids_send, ids_recv, beside_z(j)).start()
            return c

        lax.fori_loop(1, depth, send, 0)

    tile = 256

    def crowding(start, count):
        blk = table[pl.ds(start, count), :]
        b32 = blk.astype(F32)
        query = row_of(0.5 * jnp.sum(b32 * b32, axis=1, keepdims=True))
        acc_w = jnp.zeros((8, count), F32)
        acc_we = jnp.zeros((8, count), F32)
        for t in range(0, 2 * head_dev, tile):
            dots = lax.dot_general(
                heads[t : t + tile, :], blk, NT, preferred_element_type=F32
            )
            hs = jnp.concatenate([half_sq[t : t + tile, :]] * (count // 128), axis=1)
            u = (hs + query) - dots
            r = 1.0 / (u + scale)
            w = r * r
            we = w * u
            acc_w += jnp.sum(w.reshape(tile // 8, 8, count), axis=0)
            acc_we += jnp.sum(we.reshape(tile // 8, 8, count), axis=0)
        w = (scale * scale) * jnp.sum(acc_w, axis=0, keepdims=True)
        we = scale * jnp.sum(acc_we, axis=0, keepdims=True)
        return w, we

    def send_parts(slot, w, we):
        part_out[slot] = jnp.concatenate([w, we], axis=1)
        if slot == 0:
            pltpu.make_async_copy(part_out.at[slot], part_in.at[y], part_recv).start()
        else:
            remote(
                part_out.at[slot],
                part_in.at[y],
                part_send,
                part_recv,
                (chip(SLOTS[slot]) * 2 + core, me),
            ).start()

    def unit(first, count):
        w, we = crowding(first * block, count * block)
        for i in reversed(range(count)):
            lanes = slice(i * block, (i + 1) * block)
            send_parts(first + i, w[:, lanes], we[:, lanes])

    def pick_rows():
        others = ids_all.at[pl.ds(0, depth - 1)]
        pltpu.make_async_copy(others, others, ids_recv).wait()
        ids = ids_all[...].reshape(members, near)
        owner = ids // head_dev
        local = (ids - owner * head_dev).astype(F32)
        listed = owner == me
        before = (
            lax.broadcasted_iota(jnp.int32, (near, near), 0)
            < lax.broadcasted_iota(jnp.int32, (near, near), 1)
        ).astype(F32)
        rank = jnp.dot(
            listed.astype(F32).astype(BF16), before.astype(BF16), preferred_element_type=F32
        )
        columns = []
        for r in range(MOST):
            hit = jnp.where(listed & (rank == float(r)), local + 1.0, 0.0)
            columns.append(jnp.sum(hit, axis=1, keepdims=True) - 1.0)
        column = jnp.concatenate(columns, axis=0)
        slots = MOST * members
        picked = jnp.zeros((slots, width), F32)
        for t in range(head_dev // tile):
            at = pl.ds(pl.multiple_of(held + t * tile, tile), tile)
            lane = (lax.broadcasted_iota(jnp.int32, (slots, tile), 1) + t * tile).astype(F32)
            onehot = (lane == column).astype(F32).astype(BF16)
            picked += jnp.dot(onehot, heads[at, :], preferred_element_type=F32)
        picked = picked.astype(BF16)
        cut = row_out.shape[2]
        place = lax.broadcasted_iota(jnp.int32, (members * 16, slots), 0)
        slot = lax.broadcasted_iota(jnp.int32, (members * 16, slots), 1)
        target = lax.rem(slot, members) * 16 + slot // members
        packed = jnp.zeros((members * 16, cut), F32)
        for c in range(width // cut):
            move = (place == target + MOST * c).astype(F32).astype(BF16)
            packed += jnp.dot(
                move, picked[:, c * cut : (c + 1) * cut], preferred_element_type=F32
            )
        row_out[...] = packed.astype(BF16).reshape(members, 16, cut)
        pltpu.make_async_copy(row_out.at[z * across + x], row_in.at[me], row_recv).start()

        for dx, dz in far_first:
            to_x = lax.rem(x + dx, across)
            to_z = lax.rem(z + dz, depth)
            remote(
                row_out.at[to_z * across + to_x],
                row_in.at[me],
                row_send,
                row_recv,
                (here, to_x * depth + to_z),
            ).start()

    def finish_rows():
        own_ids.wait()
        own_vec.wait()
        pltpu.make_async_copy(row_in, row_in, row_recv).wait()
        cut = row_in.shape[2]
        owner = jnp.broadcast_to((ids_ref[...] // head_dev).astype(F32), (near, near))
        i = lax.broadcasted_iota(jnp.int32, (near, near), 0)
        j = lax.broadcasted_iota(jnp.int32, (near, near), 1)
        column = jnp.sum(jnp.where(i == j, owner, 0.0), axis=1, keepdims=True)
        rank = jnp.sum(
            jnp.where((owner == column) & (j < i), 1.0, 0.0), axis=1, keepdims=True
        )
        got = row_in[...].reshape(members * 16, cut)
        lane = lax.broadcasted_iota(jnp.int32, (near, members * 16), 1).astype(F32)
        want = column * 16.0 + rank
        dots = jnp.zeros((near, posts), F32)
        row_sq = jnp.zeros((near, 1), F32)
        vec_sq = jnp.zeros((posts, 1), F32)
        for c in range(width // cut):
            choose = (lane == want + float(MOST * c)).astype(F32).astype(BF16)
            rows = jnp.dot(choose, got, preferred_element_type=F32)
            vec = vec_ref[:, c * cut : (c + 1) * cut]
            v32 = vec.astype(F32)
            row_sq += jnp.sum(rows * rows, axis=1, keepdims=True)
            vec_sq += jnp.sum(v32 * v32, axis=1, keepdims=True)
            dots += lax.dot_general(rows.astype(BF16), vec, NT, preferred_element_type=F32)
        result_ref[0:near, :] = (row_sq + row_of(vec_sq) - 2.0 * dots) / width

    heads_copy.wait()
    square_heads(held)
    for slot, after, step in ((1, 5, 2), (2, 6, -2)):
        arrive(slot)
        spread_out(slot)
        next_hop(slot, after, step)
    know_all()
    for slot in (3, 4):
        arrive(slot)
        spread_out(slot)
    next_hop(3 + core, ACROSS, 2 - 4 * core)
    send_lists()
    for slot in (5, 6, ACROSS):
        arrive(slot)
        spread_out(slot)
    twin_heads.wait_recv()
    square_heads(twin_held)
    own.wait()
    for slot in (1, 2, 3):
        whole(slot)
    unit(0, 4)
    for slot in (4, 5, 6, ACROSS):
        whole(slot)
    unit(4, 4)
    pick_rows()

    pltpu.make_async_copy(part_in, part_in, part_recv).wait()
    sum_out[...] = jnp.sum(part_in[...], axis=0)
    pltpu.make_async_copy(sum_out, sum_in.at[me], sum_recv).start()

    for dx, dz in far_first:
        to = lax.rem(x + dx, across) * depth + lax.rem(z + dz, depth)
        remote(sum_out, sum_in.at[me], sum_send, sum_recv, (here, to)).start()
    finish_rows()
    pltpu.make_async_copy(sum_in, sum_in, sum_recv).wait()
    total = jnp.sum(sum_in[...], axis=0)
    w = total[:, 0:block]
    we = total[:, block : 2 * block]
    result_ref[near : near + 1, 0:block] = jnp.log(w / float(total_heads))
    result_ref[near : near + 1, 64 : 64 + block] = we / w

    for sem, count in ((ring_send, 7 * piece), (side_send, 21 * piece)):
        sent = table.at[pl.ds(0, count)]
        pltpu.make_async_copy(sent, sent, sem).wait()
    twin_heads.wait_send()
    others = pl.ds(0, members - 1)
    lines = ids_all.at[0, pl.ds(0, across - 1)]
    pltpu.make_async_copy(lines, lines, line_send).wait()
    lists = ids_all.at[pl.ds(0, depth - 1)]
    pltpu.make_async_copy(lists, lists, ids_send).wait()
    pltpu.make_async_copy(row_in.at[others], row_in.at[others], row_send).wait()
    pltpu.make_async_copy(sum_in.at[others], sum_in.at[others], sum_send).wait()
    others = pl.ds(0, chips - 1)
    pltpu.make_async_copy(part_in.at[others], part_in.at[others], part_send).wait()


def part(result_ref, density_ref, spread_ref, reassign_ref):
    near, block = reassign_ref.shape[0], density_ref.shape[1]
    density_ref[...] = result_ref[near : near + 1, 0:block]
    spread_ref[...] = result_ref[near : near + 1, 64 : 64 + block]
    reassign_ref[...] = result_ref[0:near, :]


def per_device(heads, new_heads, vectors, near_ids):
    groups = lax.axis_size("group")
    members = lax.axis_size("member")
    head_dev, width = heads.shape
    block = new_heads.shape[0]
    posts = vectors.shape[1]
    near = near_ids.shape[1]
    depth = 8
    anywhere = pl.BlockSpec(memory_space=pltpu.HBM)
    vmem = pl.BlockSpec(memory_space=pltpu.VMEM)
    dma = pltpu.SemaphoreType.DMA
    result = pl.pallas_call(
        functools.partial(kernel, (groups, members, depth, head_dev * groups * members)),
        out_shape=jax.ShapeDtypeStruct((near + 8, posts), F32),
        in_specs=[anywhere] * 4,
        out_specs=vmem,
        scratch_shapes=[
            pltpu.VMEM((2 * head_dev, width), BF16),
            pltpu.VMEM((posts, width), BF16),
            pltpu.VMEM((1, near), jnp.int32),
            pltpu.VMEM((2 * head_dev, 128), F32),
            pltpu.VMEM((groups // 2 * block, width), BF16),
            pltpu.VMEM((depth, members // depth, 1, near), jnp.int32),
            pltpu.VMEM((members, 16, 256), BF16),
            pltpu.VMEM((members, 16, 256), BF16),
            pltpu.VMEM((groups // 2, 1, 2 * block), F32),
            pltpu.VMEM((groups // 2, 1, 2 * block), F32),
            pltpu.VMEM((1, 2 * block), F32),
            pltpu.VMEM((members, 1, 2 * block), F32),
            dma,
            dma((3,)),
            dma,
            dma((8,)),
            dma,
            dma((8,)),
            dma,
            dma,
            dma,
            dma,
            dma,
            dma,
            pltpu.SemaphoreType.REGULAR,
            pltpu.SemaphoreType.REGULAR((3,)),
            dma,
            dma,
            dma,
            dma,
            dma,
            dma,
        ],
        compiler_params=pltpu.CompilerParams(
            collective_id=0, has_side_effects=True, vmem_limit_bytes=60 * 1024 * 1024
        ),
    )(heads, new_heads, vectors[0], near_ids)
    density, spread, reassign = pl.pallas_call(
        part,
        out_shape=(
            jax.ShapeDtypeStruct((1, block), F32),
            jax.ShapeDtypeStruct((1, block), F32),
            jax.ShapeDtypeStruct((near, posts), F32),
        ),
        in_specs=[vmem],
        out_specs=(vmem, vmem, vmem),
    )(result)
    return density[0], spread[0], reassign[None]


def solution(mesh):
    placed = (
        P(("group", "member"), None),
        P("group", None),
        P(("group", "member"), None, None),
        P(("group", "member"), None),
    )
    return jax.shard_map(
        per_device,
        mesh=mesh,
        in_specs=placed,
        out_specs=(P("group"), P("group"), P(("group", "member"), None, None)),
        check_vma=False,
    )
```

```python
import functools

import jax
import jax.numpy as jnp
from jax import lax
from jax.experimental import pallas as pl
from jax.experimental.pallas import tpu as pltpu
from jax.sharding import PartitionSpec as P

F32 = jnp.float32
BF16 = jnp.bfloat16
MOST = 4
SHADES = 4
SLOTS = (0, -1, 1, -2, 2, -3, 3, 4)
ACROSS = 7
NT = (((1,), (1,)), ((), ()))


def row_of(column):
    n = column.shape[0]
    return jnp.transpose(jnp.broadcast_to(column, (n, 128)))[0:1, :]


def kernel(
    shape,
    heads_hbm,
    new_ref,
    vec_hbm,
    ids_hbm,
    result_ref,
    heads,
    vec_ref,
    ids_ref,
    half_sq,
    table,
    ids_all,
    row_out,
    row_in,
    part_out,
    part_in,
    sum_out,
    sum_in,
    heads_sem,
    own_sem,
    ring_send,
    ring_recv,
    side_send,
    side_recv,
    twin_send,
    twin_recv,
    line_send,
    line_recv,
    ids_send,
    ids_recv,
    know_x,
    know_z,
    row_send,
    row_recv,
    part_send,
    part_recv,
    sum_send,
    sum_recv,
):
    groups, members, depth, total_heads = shape
    chips = groups // 2
    across = members // depth
    here = lax.axis_index("group")
    me = lax.axis_index("member")
    y = here // 2
    core = here % 2
    x = me // depth
    z = me % depth
    twin = y * 2 + (1 - core)
    head_dev, width = heads_hbm.shape
    block = new_ref.shape[0]
    near = ids_ref.shape[1]
    posts = vec_ref.shape[0]
    scale = width / 2.0
    far_first = sorted(
        [(i, j) for i in range(across) for j in range(depth) if i or j],
        key=lambda d: -min(d[0], across - d[0]) - min(d[1], depth - d[1]),
    )
    shade = lax.rem(x + 2 * z, SHADES)
    piece = block // SHADES

    def chip(step):
        return lax.rem(y + step + chips, chips)

    def beside_x(step):
        return (here, lax.rem(x + step + across, across) * depth + z)

    def beside_z(step):
        return (here, x * depth + lax.rem(z + step + depth, depth))

    def signal(sem, device):
        pl.semaphore_signal(sem, inc=1, device_id=device, device_id_type=pl.DeviceIdType.MESH)

    def remote(src, dst, send, recv, device):
        return pltpu.make_async_remote_copy(
            src_ref=src,
            dst_ref=dst,
            send_sem=send,
            recv_sem=recv,
            device_id=device,
            device_id_type=pl.DeviceIdType.MESH,
        )

    barrier = pltpu.get_barrier_semaphore()
    for device in (
        (chip(1) * 2 + core, me),
        (chip(-1) * 2 + core, me),
        (chip(2) * 2 + core, me),
        (chip(-2) * 2 + core, me),
        (twin, me),
        beside_z(1),
        beside_z(-1),
        beside_x(1),
        beside_x(-1),
    ):
        signal(barrier, device)

    held = pl.multiple_of(core * head_dev, head_dev)
    twin_held = pl.multiple_of((1 - core) * head_dev, head_dev)
    heads_copy = pltpu.make_async_copy(heads_hbm, heads.at[pl.ds(held, head_dev)], heads_sem)
    own = pltpu.make_async_copy(new_ref, table.at[pl.ds(0, block)], own_sem.at[0])
    own_vec = pltpu.make_async_copy(vec_hbm, vec_ref, own_sem.at[1])
    own_ids = pltpu.make_async_copy(ids_hbm, ids_ref, own_sem.at[2])
    own_ids.start()
    own.start()
    heads_copy.start()
    own_vec.start()

    def rows_at(slot, first, count):
        return table.at[pl.ds(pl.multiple_of(slot * block + first, 16), count)]

    def hop(src, slot, step):
        remote(
            src,
            rows_at(slot, shade * piece, piece),
            ring_send,
            ring_recv.at[slot],
            (chip(step) * 2 + core, me),
        ).start()

    def first_hop(slot):
        hop(rows_at(0, shade * piece, piece), slot, -SLOTS[slot])

    def next_hop(slot, after, step):
        hop(rows_at(slot, shade * piece, piece), after, step)

    def arrive(slot):
        mine = rows_at(slot, shade * piece, piece)
        pltpu.make_async_copy(mine, mine, ring_recv.at[slot]).wait()

    def spread_out(slot):
        mine = rows_at(slot, shade * piece, piece)
        if slot == ACROSS:
            way = 1 - 2 * core
        else:
            way = -1 if SLOTS[slot] > 0 else 1
        for device in (beside_x(1), beside_x(-1), beside_z(way)):
            remote(mine, mine, side_send, side_recv.at[slot], device).start()

    def whole(slot):
        others = rows_at(slot, 0, block - piece)
        pltpu.make_async_copy(others, others, side_recv.at[slot]).wait()

    own.wait()
    pl.semaphore_wait(barrier, 9)

    for slot in (3, 4, 1, 2):
        first_hop(slot)
    signal(know_x, beside_x(-1))
    for way in (1, -1):
        signal(know_z.at[0], beside_z(way))

    line_own = pltpu.make_async_copy(ids_hbm, ids_all.at[z, x], line_recv)
    line_own.start()

    def send_line(step):
        remote(ids_hbm, ids_all.at[z, x], line_send, line_recv, beside_x(step)).start()

    send_line(1)
    send_line(-1)
    twin_heads = remote(
        heads_hbm, heads.at[pl.ds(held, head_dev)], twin_send, twin_recv, (twin, me)
    )
    twin_heads.start()
    pl.semaphore_wait(know_x, 1)
    for step in range(2, across - 1):
        send_line(step)
    pl.semaphore_wait(know_z.at[0], 2)
    for way in (1, -1):
        signal(know_z.at[1], beside_z(way))

    def square_heads(first):
        def square(t, c):
            at = pl.ds(pl.multiple_of(first + t * tile, tile), tile)
            h = heads[at, :].astype(F32)
            half_sq[at, :] = jnp.broadcast_to(
                0.5 * jnp.sum(h * h, axis=1, keepdims=True), (tile, 128)
            )
            return c

        lax.fori_loop(0, head_dev // tile, square, 0)

    def know_all():
        pl.semaphore_wait(know_z.at[1], 2)
        for way in (1, -1):
            signal(know_z.at[2], beside_z(way))

    def send_lists():
        pltpu.make_async_copy(ids_all.at[z], ids_all.at[z], line_recv).wait()
        pl.semaphore_wait(know_z.at[2], 2)

        def send(j, c):
            remote(ids_all.at[z], ids_all.at[z], ids_send, ids_recv, beside_z(j)).start()
            return c

        lax.fori_loop(1, depth, send, 0)

    tile = 256

    def crowding(start, count):
        blk = table[pl.ds(start, count), :]
        b32 = blk.astype(F32)
        query = row_of(0.5 * jnp.sum(b32 * b32, axis=1, keepdims=True))
        acc_w = jnp.zeros((8, count), F32)
        acc_we = jnp.zeros((8, count), F32)
        for t in range(0, 2 * head_dev, tile):
            dots = lax.dot_general(
                heads[t : t + tile, :], blk, NT, preferred_element_type=F32
            )
            hs = jnp.concatenate([half_sq[t : t + tile, :]] * (count // 128), axis=1)
            u = (hs + query) - dots
            r = 1.0 / (u + scale)
            w = r * r
            we = w * u
            acc_w += jnp.sum(w.reshape(tile // 8, 8, count), axis=0)
            acc_we += jnp.sum(we.reshape(tile // 8, 8, count), axis=0)
        w = (scale * scale) * jnp.sum(acc_w, axis=0, keepdims=True)
        we = scale * jnp.sum(acc_we, axis=0, keepdims=True)
        return w, we

    def send_parts(slot, w, we):
        part_out[slot] = jnp.concatenate([w, we], axis=1)
        if slot == 0:
            pltpu.make_async_copy(part_out.at[slot], part_in.at[y], part_recv).start()
        else:
            remote(
                part_out.at[slot],
                part_in.at[y],
                part_send,
                part_recv,
                (chip(SLOTS[slot]) * 2 + core, me),
            ).start()

    def unit(first, count):
        w, we = crowding(first * block, count * block)
        for i in reversed(range(count)):
            lanes = slice(i * block, (i + 1) * block)
            send_parts(first + i, w[:, lanes], we[:, lanes])

    def pick_rows():
        others = ids_all.at[pl.ds(0, depth - 1)]
        pltpu.make_async_copy(others, others, ids_recv).wait()
        ids = ids_all[...].reshape(members, near)
        owner = ids // head_dev
        local = (ids - owner * head_dev).astype(F32)
        listed = owner == me
        before = (
            lax.broadcasted_iota(jnp.int32, (near, near), 0)
            < lax.broadcasted_iota(jnp.int32, (near, near), 1)
        ).astype(F32)
        rank = jnp.dot(
            listed.astype(F32).astype(BF16), before.astype(BF16), preferred_element_type=F32
        )
        columns = []
        for r in range(MOST):
            hit = jnp.where(listed & (rank == float(r)), local + 1.0, 0.0)
            columns.append(jnp.sum(hit, axis=1, keepdims=True) - 1.0)
        column = jnp.concatenate(columns, axis=0)
        slots = MOST * members
        picked = jnp.zeros((slots, width), F32)
        for t in range(head_dev // tile):
            at = pl.ds(pl.multiple_of(held + t * tile, tile), tile)
            lane = (lax.broadcasted_iota(jnp.int32, (slots, tile), 1) + t * tile).astype(F32)
            onehot = (lane == column).astype(F32).astype(BF16)
            picked += jnp.dot(onehot, heads[at, :], preferred_element_type=F32)
        picked = picked.astype(BF16)
        cut = row_out.shape[2]
        place = lax.broadcasted_iota(jnp.int32, (members * 16, slots), 0)
        slot = lax.broadcasted_iota(jnp.int32, (members * 16, slots), 1)
        target = lax.rem(slot, members) * 16 + slot // members
        packed = jnp.zeros((members * 16, cut), F32)
        for c in range(width // cut):
            move = (place == target + MOST * c).astype(F32).astype(BF16)
            packed += jnp.dot(
                move, picked[:, c * cut : (c + 1) * cut], preferred_element_type=F32
            )
        row_out[...] = packed.astype(BF16).reshape(members, 16, cut)
        pltpu.make_async_copy(row_out.at[z * across + x], row_in.at[me], row_recv).start()

        for dx, dz in far_first:
            to_x = lax.rem(x + dx, across)
            to_z = lax.rem(z + dz, depth)
            remote(
                row_out.at[to_z * across + to_x],
                row_in.at[me],
                row_send,
                row_recv,
                (here, to_x * depth + to_z),
            ).start()

    def finish_rows():
        own_ids.wait()
        own_vec.wait()
        cut = row_in.shape[2]
        owner = jnp.broadcast_to((ids_ref[...] // head_dev).astype(F32), (near, near))
        i = lax.broadcasted_iota(jnp.int32, (near, near), 0)
        j = lax.broadcasted_iota(jnp.int32, (near, near), 1)
        column = jnp.sum(jnp.where(i == j, owner, 0.0), axis=1, keepdims=True)
        rank = jnp.sum(
            jnp.where((owner == column) & (j < i), 1.0, 0.0), axis=1, keepdims=True
        )
        lane = lax.broadcasted_iota(jnp.int32, (near, members * 16), 1).astype(F32)
        want = column * 16.0 + rank
        starts = range(0, width, cut)
        choose = [
            (lane == want + float(MOST * c)).astype(F32).astype(BF16)
            for c in range(len(starts))
        ]
        v32 = vec_ref[...].astype(F32)
        vec_sq = row_of(jnp.sum(v32 * v32, axis=1, keepdims=True))
        pltpu.make_async_copy(row_in, row_in, row_recv).wait()
        got = row_in[...].reshape(members * 16, cut)
        dots = jnp.zeros((near, posts), F32)
        row_sq = jnp.zeros((near, 1), F32)
        for c, start in enumerate(starts):
            rows = jnp.dot(choose[c], got, preferred_element_type=F32)
            row_sq += jnp.sum(rows * rows, axis=1, keepdims=True)
            dots += lax.dot_general(
                rows.astype(BF16),
                vec_ref[:, start : start + cut],
                NT,
                preferred_element_type=F32,
            )
        result_ref[0:near, :] = (row_sq + vec_sq - 2.0 * dots) / width

    heads_copy.wait()
    square_heads(held)
    for slot in (1, 2):
        arrive(slot)
        spread_out(slot)
    know_all()
    for slot, after, step in ((3, 5, 1), (4, 6, -1)):
        arrive(slot)
        next_hop(slot, after, step)
    next_hop(3 + core, ACROSS, 2 - 4 * core)
    for slot in (3, 4):
        spread_out(slot)
    for slot in (5, 6, ACROSS):
        arrive(slot)
        spread_out(slot)
    send_lists()
    twin_heads.wait_recv()
    square_heads(twin_held)
    for slot in (1, 2, 3):
        whole(slot)
    unit(0, 4)
    for slot in (4, 5, 6, ACROSS):
        whole(slot)
    unit(4, 4)
    pick_rows()

    pltpu.make_async_copy(part_in, part_in, part_recv).wait()
    sum_out[...] = jnp.sum(part_in[...], axis=0)
    pltpu.make_async_copy(sum_out, sum_in.at[me], sum_recv).start()

    for dx, dz in far_first:
        to = lax.rem(x + dx, across) * depth + lax.rem(z + dz, depth)
        remote(sum_out, sum_in.at[me], sum_send, sum_recv, (here, to)).start()
    finish_rows()
    pltpu.make_async_copy(sum_in, sum_in, sum_recv).wait()
    total = jnp.sum(sum_in[...], axis=0)
    w = total[:, 0:block]
    we = total[:, block : 2 * block]
    result_ref[near : near + 1, 0:block] = jnp.log(w / float(total_heads))
    result_ref[near : near + 1, 64 : 64 + block] = we / w

    for sem, count in ((ring_send, 7 * piece), (side_send, 21 * piece)):
        sent = table.at[pl.ds(0, count)]
        pltpu.make_async_copy(sent, sent, sem).wait()
    twin_heads.wait_send()
    others = pl.ds(0, members - 1)
    lines = ids_all.at[0, pl.ds(0, across - 1)]
    pltpu.make_async_copy(lines, lines, line_send).wait()
    lists = ids_all.at[pl.ds(0, depth - 1)]
    pltpu.make_async_copy(lists, lists, ids_send).wait()
    pltpu.make_async_copy(row_in.at[others], row_in.at[others], row_send).wait()
    pltpu.make_async_copy(sum_in.at[others], sum_in.at[others], sum_send).wait()
    others = pl.ds(0, chips - 1)
    pltpu.make_async_copy(part_in.at[others], part_in.at[others], part_send).wait()


def part(result_ref, density_ref, spread_ref, reassign_ref):
    near, block = reassign_ref.shape[0], density_ref.shape[1]
    density_ref[...] = result_ref[near : near + 1, 0:block]
    spread_ref[...] = result_ref[near : near + 1, 64 : 64 + block]
    reassign_ref[...] = result_ref[0:near, :]


def per_device(heads, new_heads, vectors, near_ids):
    groups = lax.axis_size("group")
    members = lax.axis_size("member")
    head_dev, width = heads.shape
    block = new_heads.shape[0]
    posts = vectors.shape[1]
    near = near_ids.shape[1]
    depth = 8
    anywhere = pl.BlockSpec(memory_space=pltpu.HBM)
    vmem = pl.BlockSpec(memory_space=pltpu.VMEM)
    dma = pltpu.SemaphoreType.DMA
    result = pl.pallas_call(
        functools.partial(kernel, (groups, members, depth, head_dev * groups * members)),
        out_shape=jax.ShapeDtypeStruct((near + 8, posts), F32),
        in_specs=[anywhere] * 4,
        out_specs=vmem,
        scratch_shapes=[
            pltpu.VMEM((2 * head_dev, width), BF16),
            pltpu.VMEM((posts, width), BF16),
            pltpu.VMEM((1, near), jnp.int32),
            pltpu.VMEM((2 * head_dev, 128), F32),
            pltpu.VMEM((groups // 2 * block, width), BF16),
            pltpu.VMEM((depth, members // depth, 1, near), jnp.int32),
            pltpu.VMEM((members, 16, 256), BF16),
            pltpu.VMEM((members, 16, 256), BF16),
            pltpu.VMEM((groups // 2, 1, 2 * block), F32),
            pltpu.VMEM((groups // 2, 1, 2 * block), F32),
            pltpu.VMEM((1, 2 * block), F32),
            pltpu.VMEM((members, 1, 2 * block), F32),
            dma,
            dma((3,)),
            dma,
            dma((8,)),
            dma,
            dma((8,)),
            dma,
            dma,
            dma,
            dma,
            dma,
            dma,
            pltpu.SemaphoreType.REGULAR,
            pltpu.SemaphoreType.REGULAR((3,)),
            dma,
            dma,
            dma,
            dma,
            dma,
            dma,
        ],
        compiler_params=pltpu.CompilerParams(
            collective_id=0, has_side_effects=True, vmem_limit_bytes=60 * 1024 * 1024
        ),
    )(heads, new_heads, vectors[0], near_ids)
    density, spread, reassign = pl.pallas_call(
        part,
        out_shape=(
            jax.ShapeDtypeStruct((1, block), F32),
            jax.ShapeDtypeStruct((1, block), F32),
            jax.ShapeDtypeStruct((near, posts), F32),
        ),
        in_specs=[vmem],
        out_specs=(vmem, vmem, vmem),
    )(result)
    return density[0], spread[0], reassign[None]


def solution(mesh):
    placed = (
        P(("group", "member"), None),
        P("group", None),
        P(("group", "member"), None, None),
        P(("group", "member"), None),
    )
    return jax.shard_map(
        per_device,
        mesh=mesh,
        in_specs=placed,
        out_specs=(P("group"), P("group"), P(("group", "member"), None, None)),
        check_vma=False,
    )
```

```python
import functools

import jax
import jax.numpy as jnp
from jax import lax
from jax.experimental import pallas as pl
from jax.experimental.pallas import tpu as pltpu
from jax.sharding import PartitionSpec as P

F32 = jnp.float32
BF16 = jnp.bfloat16
MOST = 4
SHADES = 4
SLOTS = (0, -1, 1, -2, 2, -3, 3, 4)
ACROSS = 7
NT = (((1,), (1,)), ((), ()))


def row_of(column):
    n = column.shape[0]
    return jnp.transpose(jnp.broadcast_to(column, (n, 128)))[0:1, :]


def kernel(
    shape,
    heads_hbm,
    new_ref,
    vec_hbm,
    ids_hbm,
    result_ref,
    heads,
    vec_ref,
    ids_ref,
    half_sq,
    table,
    ids_all,
    row_out,
    row_in,
    part_out,
    part_in,
    sum_out,
    sum_in,
    heads_sem,
    own_sem,
    ring_send,
    ring_recv,
    side_send,
    side_recv,
    twin_send,
    twin_recv,
    line_send,
    line_recv,
    ids_send,
    ids_recv,
    know_x,
    know_z,
    row_send,
    row_recv,
    part_send,
    part_recv,
    sum_send,
    sum_recv,
):
    groups, members, depth, total_heads = shape
    chips = groups // 2
    across = members // depth
    here = lax.axis_index("group")
    me = lax.axis_index("member")
    y = here // 2
    core = here % 2
    x = me // depth
    z = me % depth
    twin = y * 2 + (1 - core)
    head_dev, width = heads_hbm.shape
    block = new_ref.shape[0]
    near = ids_ref.shape[1]
    posts = vec_ref.shape[0]
    scale = width / 2.0
    far_first = sorted(
        [(i, j) for i in range(across) for j in range(depth) if i or j],
        key=lambda d: -min(d[0], across - d[0]) - min(d[1], depth - d[1]),
    )
    shade = lax.rem(x + 2 * z, SHADES)
    piece = block // SHADES

    def chip(step):
        return lax.rem(y + step + chips, chips)

    def beside_x(step):
        return (here, lax.rem(x + step + across, across) * depth + z)

    def beside_z(step):
        return (here, x * depth + lax.rem(z + step + depth, depth))

    def signal(sem, device):
        pl.semaphore_signal(sem, inc=1, device_id=device, device_id_type=pl.DeviceIdType.MESH)

    def remote(src, dst, send, recv, device):
        return pltpu.make_async_remote_copy(
            src_ref=src,
            dst_ref=dst,
            send_sem=send,
            recv_sem=recv,
            device_id=device,
            device_id_type=pl.DeviceIdType.MESH,
        )

    barrier = pltpu.get_barrier_semaphore()
    for device in (
        (chip(1) * 2 + core, me),
        (chip(-1) * 2 + core, me),
        (chip(2) * 2 + core, me),
        (chip(-2) * 2 + core, me),
        (twin, me),
        beside_z(1),
        beside_z(-1),
        beside_x(1),
        beside_x(-1),
    ):
        signal(barrier, device)

    held = pl.multiple_of(core * head_dev, head_dev)
    twin_held = pl.multiple_of((1 - core) * head_dev, head_dev)
    heads_copy = pltpu.make_async_copy(heads_hbm, heads.at[pl.ds(held, head_dev)], heads_sem)
    own = pltpu.make_async_copy(new_ref, table.at[pl.ds(0, block)], own_sem.at[0])
    own_vec = pltpu.make_async_copy(vec_hbm, vec_ref, own_sem.at[1])
    own_ids = pltpu.make_async_copy(ids_hbm, ids_ref, own_sem.at[2])
    own_ids.start()
    own.start()
    heads_copy.start()
    own_vec.start()

    def rows_at(slot, first, count):
        return table.at[pl.ds(pl.multiple_of(slot * block + first, 16), count)]

    def hop(src, slot, step):
        remote(
            src,
            rows_at(slot, shade * piece, piece),
            ring_send,
            ring_recv.at[slot],
            (chip(step) * 2 + core, me),
        ).start()

    def first_hop(slot):
        hop(rows_at(0, shade * piece, piece), slot, -SLOTS[slot])

    def next_hop(slot, after, step):
        hop(rows_at(slot, shade * piece, piece), after, step)

    def arrive(slot):
        mine = rows_at(slot, shade * piece, piece)
        pltpu.make_async_copy(mine, mine, ring_recv.at[slot]).wait()

    def spread_out(slot):
        mine = rows_at(slot, shade * piece, piece)
        if slot == ACROSS:
            way = 1 - 2 * core
        else:
            way = -1 if SLOTS[slot] > 0 else 1
        for device in (beside_x(1), beside_x(-1), beside_z(way)):
            remote(mine, mine, side_send, side_recv.at[slot], device).start()

    def whole(slot):
        others = rows_at(slot, 0, block - piece)
        pltpu.make_async_copy(others, others, side_recv.at[slot]).wait()

    own.wait()
    pl.semaphore_wait(barrier, 9)

    for slot in (3, 4, 1, 2):
        first_hop(slot)
    signal(know_x, beside_x(-1))
    for way in (1, -1):
        signal(know_z.at[0], beside_z(way))

    line_own = pltpu.make_async_copy(ids_hbm, ids_all.at[z, x], line_recv)
    line_own.start()

    def send_line(step):
        remote(ids_hbm, ids_all.at[z, x], line_send, line_recv, beside_x(step)).start()

    send_line(1)
    send_line(-1)
    twin_heads = remote(
        heads_hbm, heads.at[pl.ds(held, head_dev)], twin_send, twin_recv, (twin, me)
    )
    twin_heads.start()
    pl.semaphore_wait(know_x, 1)
    for step in range(2, across - 1):
        send_line(step)
    pl.semaphore_wait(know_z.at[0], 2)
    for way in (1, -1):
        signal(know_z.at[1], beside_z(way))

    def square_heads(first):
        def square(t, c):
            at = pl.ds(pl.multiple_of(first + t * tile, tile), tile)
            h = heads[at, :].astype(F32)
            half_sq[at, :] = jnp.broadcast_to(
                0.5 * jnp.sum(h * h, axis=1, keepdims=True), (tile, 128)
            )
            return c

        lax.fori_loop(0, head_dev // tile, square, 0)

    def know_all():
        pl.semaphore_wait(know_z.at[1], 2)
        for way in (1, -1):
            signal(know_z.at[2], beside_z(way))

    def send_lists():
        pltpu.make_async_copy(ids_all.at[z], ids_all.at[z], line_recv).wait()
        pl.semaphore_wait(know_z.at[2], 2)

        def send(j, c):
            remote(ids_all.at[z], ids_all.at[z], ids_send, ids_recv, beside_z(j)).start()
            return c

        lax.fori_loop(1, depth, send, 0)

    tile = 256

    def crowding(start, count, between):
        blk = table[pl.ds(start, count), :]
        b32 = blk.astype(F32)
        query = row_of(0.5 * jnp.sum(b32 * b32, axis=1, keepdims=True))
        acc_w = jnp.zeros((8, count), F32)
        acc_we = jnp.zeros((8, count), F32)
        for t in range(0, 2 * head_dev, tile):
            if t == head_dev:
                between()
            first = held if t < head_dev else twin_held
            at = pl.ds(pl.multiple_of(first + t % head_dev, tile), tile)
            dots = lax.dot_general(heads[at, :], blk, NT, preferred_element_type=F32)
            hs = jnp.concatenate([half_sq[at, :]] * (count // 128), axis=1)
            u = (hs + query) - dots
            r = 1.0 / (u + scale)
            w = r * r
            we = w * u
            acc_w += jnp.sum(w.reshape(tile // 8, 8, count), axis=0)
            acc_we += jnp.sum(we.reshape(tile // 8, 8, count), axis=0)
        w = (scale * scale) * jnp.sum(acc_w, axis=0, keepdims=True)
        we = scale * jnp.sum(acc_we, axis=0, keepdims=True)
        return w, we

    def send_parts(slot, w, we):
        part_out[slot] = jnp.concatenate([w, we], axis=1)
        if slot == 0:
            pltpu.make_async_copy(part_out.at[slot], part_in.at[y], part_recv).start()
        else:
            remote(
                part_out.at[slot],
                part_in.at[y],
                part_send,
                part_recv,
                (chip(SLOTS[slot]) * 2 + core, me),
            ).start()

    def unit(first, count, between):
        w, we = crowding(first * block, count * block, between)
        for i in reversed(range(count)):
            lanes = slice(i * block, (i + 1) * block)
            send_parts(first + i, w[:, lanes], we[:, lanes])

    def pick_rows():
        others = ids_all.at[pl.ds(0, depth - 1)]
        pltpu.make_async_copy(others, others, ids_recv).wait()
        ids = ids_all[...].reshape(members, near)
        owner = ids // head_dev
        local = (ids - owner * head_dev).astype(F32)
        listed = owner == me
        before = (
            lax.broadcasted_iota(jnp.int32, (near, near), 0)
            < lax.broadcasted_iota(jnp.int32, (near, near), 1)
        ).astype(F32)
        rank = jnp.dot(
            listed.astype(F32).astype(BF16), before.astype(BF16), preferred_element_type=F32
        )
        columns = []
        for r in range(MOST):
            hit = jnp.where(listed & (rank == float(r)), local + 1.0, 0.0)
            columns.append(jnp.sum(hit, axis=1, keepdims=True) - 1.0)
        column = jnp.concatenate(columns, axis=0)
        slots = MOST * members
        picked = jnp.zeros((slots, width), F32)
        for t in range(head_dev // tile):
            at = pl.ds(pl.multiple_of(held + t * tile, tile), tile)
            lane = (lax.broadcasted_iota(jnp.int32, (slots, tile), 1) + t * tile).astype(F32)
            onehot = (lane == column).astype(F32).astype(BF16)
            picked += jnp.dot(onehot, heads[at, :], preferred_element_type=F32)
        picked = picked.astype(BF16)
        cut = row_out.shape[2]
        place = lax.broadcasted_iota(jnp.int32, (members * 16, slots), 0)
        slot = lax.broadcasted_iota(jnp.int32, (members * 16, slots), 1)
        target = lax.rem(slot, members) * 16 + slot // members
        packed = jnp.zeros((members * 16, cut), F32)
        for c in range(width // cut):
            move = (place == target + MOST * c).astype(F32).astype(BF16)
            packed += jnp.dot(
                move, picked[:, c * cut : (c + 1) * cut], preferred_element_type=F32
            )
        row_out[...] = packed.astype(BF16).reshape(members, 16, cut)
        pltpu.make_async_copy(row_out.at[z * across + x], row_in.at[me], row_recv).start()

        for dx, dz in far_first:
            to_x = lax.rem(x + dx, across)
            to_z = lax.rem(z + dz, depth)
            remote(
                row_out.at[to_z * across + to_x],
                row_in.at[me],
                row_send,
                row_recv,
                (here, to_x * depth + to_z),
            ).start()

    def finish_rows():
        own_ids.wait()
        own_vec.wait()
        cut = row_in.shape[2]
        owner = jnp.broadcast_to((ids_ref[...] // head_dev).astype(F32), (near, near))
        i = lax.broadcasted_iota(jnp.int32, (near, near), 0)
        j = lax.broadcasted_iota(jnp.int32, (near, near), 1)
        column = jnp.sum(jnp.where(i == j, owner, 0.0), axis=1, keepdims=True)
        rank = jnp.sum(
            jnp.where((owner == column) & (j < i), 1.0, 0.0), axis=1, keepdims=True
        )
        lane = lax.broadcasted_iota(jnp.int32, (near, members * 16), 1).astype(F32)
        want = column * 16.0 + rank
        starts = range(0, width, cut)
        choose = [
            (lane == want + float(MOST * c)).astype(F32).astype(BF16)
            for c in range(len(starts))
        ]
        v32 = vec_ref[...].astype(F32)
        vec_sq = row_of(jnp.sum(v32 * v32, axis=1, keepdims=True))
        pltpu.make_async_copy(row_in, row_in, row_recv).wait()
        got = row_in[...].reshape(members * 16, cut)
        dots = jnp.zeros((near, posts), F32)
        row_sq = jnp.zeros((near, 1), F32)
        for c, start in enumerate(starts):
            rows = jnp.dot(choose[c], got, preferred_element_type=F32)
            row_sq += jnp.sum(rows * rows, axis=1, keepdims=True)
            dots += lax.dot_general(
                rows.astype(BF16),
                vec_ref[:, start : start + cut],
                NT,
                preferred_element_type=F32,
            )
        result_ref[0:near, :] = (row_sq + vec_sq - 2.0 * dots) / width

    heads_copy.wait()
    square_heads(held)
    for slot in (1, 2):
        arrive(slot)
        spread_out(slot)
    know_all()
    for slot, after, step in ((3, 5, 1), (4, 6, -1)):
        arrive(slot)
        next_hop(slot, after, step)
    next_hop(3 + core, ACROSS, 2 - 4 * core)
    for slot in (3, 4):
        spread_out(slot)
    for slot in (5, 6, ACROSS):
        arrive(slot)
        spread_out(slot)
    send_lists()
    for slot in (1, 2, 3):
        whole(slot)

    def take_twin():
        twin_heads.wait_recv()
        square_heads(twin_held)

    unit(0, 4, take_twin)
    for slot in (4, 5, 6, ACROSS):
        whole(slot)
    unit(4, 4, lambda: None)
    pick_rows()

    pltpu.make_async_copy(part_in, part_in, part_recv).wait()
    sum_out[...] = jnp.sum(part_in[...], axis=0)
    pltpu.make_async_copy(sum_out, sum_in.at[me], sum_recv).start()

    for dx, dz in far_first:
        to = lax.rem(x + dx, across) * depth + lax.rem(z + dz, depth)
        remote(sum_out, sum_in.at[me], sum_send, sum_recv, (here, to)).start()
    finish_rows()
    pltpu.make_async_copy(sum_in, sum_in, sum_recv).wait()
    total = jnp.sum(sum_in[...], axis=0)
    w = total[:, 0:block]
    we = total[:, block : 2 * block]
    result_ref[near : near + 1, 0:block] = jnp.log(w / float(total_heads))
    result_ref[near : near + 1, 64 : 64 + block] = we / w

    for sem, count in ((ring_send, 7 * piece), (side_send, 21 * piece)):
        sent = table.at[pl.ds(0, count)]
        pltpu.make_async_copy(sent, sent, sem).wait()
    twin_heads.wait_send()
    others = pl.ds(0, members - 1)
    lines = ids_all.at[0, pl.ds(0, across - 1)]
    pltpu.make_async_copy(lines, lines, line_send).wait()
    lists = ids_all.at[pl.ds(0, depth - 1)]
    pltpu.make_async_copy(lists, lists, ids_send).wait()
    pltpu.make_async_copy(row_in.at[others], row_in.at[others], row_send).wait()
    pltpu.make_async_copy(sum_in.at[others], sum_in.at[others], sum_send).wait()
    others = pl.ds(0, chips - 1)
    pltpu.make_async_copy(part_in.at[others], part_in.at[others], part_send).wait()


def part(result_ref, density_ref, spread_ref, reassign_ref):
    near, block = reassign_ref.shape[0], density_ref.shape[1]
    density_ref[...] = result_ref[near : near + 1, 0:block]
    spread_ref[...] = result_ref[near : near + 1, 64 : 64 + block]
    reassign_ref[...] = result_ref[0:near, :]


def per_device(heads, new_heads, vectors, near_ids):
    groups = lax.axis_size("group")
    members = lax.axis_size("member")
    head_dev, width = heads.shape
    block = new_heads.shape[0]
    posts = vectors.shape[1]
    near = near_ids.shape[1]
    depth = 8
    anywhere = pl.BlockSpec(memory_space=pltpu.HBM)
    vmem = pl.BlockSpec(memory_space=pltpu.VMEM)
    dma = pltpu.SemaphoreType.DMA
    result = pl.pallas_call(
        functools.partial(kernel, (groups, members, depth, head_dev * groups * members)),
        out_shape=jax.ShapeDtypeStruct((near + 8, posts), F32),
        in_specs=[anywhere] * 4,
        out_specs=vmem,
        scratch_shapes=[
            pltpu.VMEM((2 * head_dev, width), BF16),
            pltpu.VMEM((posts, width), BF16),
            pltpu.VMEM((1, near), jnp.int32),
            pltpu.VMEM((2 * head_dev, 128), F32),
            pltpu.VMEM((groups // 2 * block, width), BF16),
            pltpu.VMEM((depth, members // depth, 1, near), jnp.int32),
            pltpu.VMEM((members, 16, 256), BF16),
            pltpu.VMEM((members, 16, 256), BF16),
            pltpu.VMEM((groups // 2, 1, 2 * block), F32),
            pltpu.VMEM((groups // 2, 1, 2 * block), F32),
            pltpu.VMEM((1, 2 * block), F32),
            pltpu.VMEM((members, 1, 2 * block), F32),
            dma,
            dma((3,)),
            dma,
            dma((8,)),
            dma,
            dma((8,)),
            dma,
            dma,
            dma,
            dma,
            dma,
            dma,
            pltpu.SemaphoreType.REGULAR,
            pltpu.SemaphoreType.REGULAR((3,)),
            dma,
            dma,
            dma,
            dma,
            dma,
            dma,
        ],
        compiler_params=pltpu.CompilerParams(
            collective_id=0, has_side_effects=True, vmem_limit_bytes=60 * 1024 * 1024
        ),
    )(heads, new_heads, vectors[0], near_ids)
    density, spread, reassign = pl.pallas_call(
        part,
        out_shape=(
            jax.ShapeDtypeStruct((1, block), F32),
            jax.ShapeDtypeStruct((1, block), F32),
            jax.ShapeDtypeStruct((near, posts), F32),
        ),
        in_specs=[vmem],
        out_specs=(vmem, vmem, vmem),
    )(result)
    return density[0], spread[0], reassign[None]


def solution(mesh):
    placed = (
        P(("group", "member"), None),
        P("group", None),
        P(("group", "member"), None, None),
        P(("group", "member"), None),
    )
    return jax.shard_map(
        per_device,
        mesh=mesh,
        in_specs=placed,
        out_specs=(P("group"), P("group"), P(("group", "member"), None, None)),
        check_vma=False,
    )
```
